32 devices in a mesh: group: 4 (over y, core), local: 8 (over z, x).
Axes of the slice: x: 2, y: 2, z: 4, core: 2. Of those that a mesh axis runs over, the one named last changes fastest.
Arguments:
- hidden_states: bfloat16 [4096, 3584], P(('group', 'local')), may hold values from -6 to 6
- affinity: float32 [4096, 8], P(('group', 'local')), may hold values from 0.1 to 1
- group_ids: int32 [4096, 4], P(('group', 'local')), may hold values from 0 to 3, as said below
- expert_ids: int32 [4096, 8], P(('group', 'local')), may hold values from 0 to 31, as said below
- w_gate: bfloat16 [32, 3584, 1024], P(('group', 'local')), may hold values from -0.09375 to 0.09375
- w_up: bfloat16 [32, 3584, 1024], P(('group', 'local')), may hold values from -0.09375 to 0.09375
- w_down: bfloat16 [32, 1024, 3584], P(('group', 'local')), may hold values from -0.1875 to 0.1875
Outputs:
- routed_out: bfloat16 [4096, 3584], P(('group', 'local'))
The draws below stay inside these ranges and needn't reach their ends.
Inputs may be any that keep to these rules, and one draw needn't show every extreme that they name: `group_ids`: each row names 4 different groups, and every group is named by exactly 128 of the tokens of one device. `expert_ids`: each row names 8 different experts; columns 2 j and 2 j + 1 lie in group group_ids[t, j]. Of the tokens of one device at most 40 name any one expert, and in every group some expert is named by exactly 40 tokens of every device.
All inputs are finite; a program needn't handle non-finite values.
Results may differ from the reference program's by a relative error of at most 0.007.
Values may be sent and summed in bfloat16 or wider, within the bound.
No kernel may reach another device: no remote copies, remote signals or barrier semaphores. Data moves between devices by JAX's collectives and lax.ppermute only.
A program may use at most 128 MiB of HBM per device.

```python
import math
import jax
import jax.numpy as jnp
from jax import lax

D = 3584
HID = 1024
TOP_K = 8
TOPG = 4
TOK_DEV = 128
GROUPS = 4
EXP_GROUP = 8
EXPERTS = 32
TOKENS = 4096
TOK_GRP = 128
MOST = 40


def group_counts(count_key, hot_local):
    expert_rank = jax.random.permutation(jax.random.fold_in(count_key, 1), EXP_GROUP)
    move_sizes = jax.random.randint(jax.random.fold_in(count_key, 2), (EXP_GROUP,), 0, 4)
    positions = jnp.arange(EXP_GROUP)
    total_rest = 2 * TOK_GRP - MOST
    even_share = total_rest // (EXP_GROUP - 1)
    extra_count = total_rest % (EXP_GROUP - 1)
    base_by = even_share + (positions < extra_count).astype(jnp.int32)
    pair_first = positions // 2 * 2
    pair_second = jnp.minimum(pair_first + 1, EXP_GROUP - 1)
    paired = pair_first + 1 <= EXP_GROUP - 2
    step_size = jnp.minimum(move_sizes[positions // 2], jnp.minimum(MOST - base_by[pair_first], base_by[pair_second]))
    step_size = jnp.where(paired, step_size, 0)
    adjusted = base_by + jnp.where(positions % 2 == 0, step_size, -step_size)
    hot_rank = expert_rank[hot_local]
    dense_rank = expert_rank - (expert_rank > hot_rank).astype(jnp.int32)
    counts = adjusted[jnp.clip(dense_rank, 0, EXP_GROUP - 1)]
    return jnp.where(positions == hot_local, MOST, counts).astype(jnp.int32)


def device_routes(dev_key, hot_local):
    token_rank = jax.random.permutation(jax.random.fold_in(dev_key, 1), TOK_DEV)
    group_order = jax.random.permutation(jax.random.fold_in(dev_key, 2), GROUPS)
    count_keys = jax.vmap(lambda index_g: jax.random.fold_in(dev_key, 10 + index_g))(jnp.arange(GROUPS))
    counts = jax.vmap(group_counts)(count_keys, hot_local)
    bounds = jnp.cumsum(counts, axis=1)
    slots = jnp.arange(2 * TOK_GRP)
    expert_list = jnp.sum((bounds[:, None, :] <= slots[None, :, None]).astype(jnp.int32), axis=2)
    steps_j = jnp.arange(TOPG)
    chosen = group_order[(token_rank[:, None] + steps_j[None, :]) % GROUPS]
    within = token_rank[:, None] // GROUPS * TOPG + steps_j[None, :]
    first_local = expert_list[chosen, within]
    second_local = expert_list[chosen, within + TOK_GRP]
    experts = chosen[:, :, None] * EXP_GROUP + jnp.stack([first_local, second_local], axis=2)
    return (chosen.astype(jnp.int32), experts.reshape(TOK_DEV, TOP_K).astype(jnp.int32))


def route_tables(key):
    route_key = jax.random.fold_in(key, 4242)
    hot_local = jax.random.randint(jax.random.fold_in(route_key, 1), (GROUPS,), 0, EXP_GROUP)
    dev_keys = jax.vmap(lambda index_d: jax.random.fold_in(route_key, 100 + index_d))(jnp.arange(GROUPS * EXP_GROUP))
    chosen, experts = jax.vmap(lambda dev_key: device_routes(dev_key, hot_local))(dev_keys)
    return (chosen.reshape(TOKENS, TOPG), experts.reshape(TOKENS, TOP_K))


def draw_group_ids(key, part):
    return route_tables(key)[0]


def draw_expert_ids(key, part):
    return route_tables(key)[1]


def level_of(stream_key, dims, cuts, smallest, top_value):
    level = 1.0
    for axis_at, parts in cuts:
        draws = jax.random.uniform(jax.random.fold_in(jax.random.fold_in(stream_key, 6), axis_at), (parts,), jnp.float32, smallest / len(cuts), top_value / len(cuts))
        level = level * jnp.repeat(jnp.exp(draws), dims[axis_at] // parts).reshape((-1,) + (1,) * (len(dims) - 1 - axis_at))
    return level


def gaussian(rng, shape, width, most, split=(), kind=jnp.bfloat16):
    array = jax.random.normal(rng, shape, jnp.float32) * width
    if len(split) > 0:
        array = level_of(rng, shape, split, -0.22, 0.18) * array
    return jnp.clip(array, min=-most, max=most).astype(kind)


def setup_inputs(seed: int = 0) -> dict:
    key_list = jax.random.split(jax.random.key(seed), 8)
    return {
        "hidden_states": gaussian(key_list[0], (TOKENS, D), 1.0, 6.0, ((0, 32),)),
        "affinity": jnp.clip(jnp.exp(math.log(1.0) - 2.3025851 * jax.random.uniform(key_list[1], (TOKENS, TOP_K), jnp.float32) ** level_of(key_list[1], (TOKENS, TOP_K), ((0, 32),), -0.2, 0.2)), 0.1, 1.0),
        "group_ids": draw_group_ids(jax.random.fold_in(key_list[7], 71), 0),
        "expert_ids": draw_expert_ids(jax.random.fold_in(key_list[7], 71), 0),
        "w_gate": gaussian(key_list[4], (EXPERTS, D, HID), D ** -0.5, 0.09375, ((0, 32),)),
        "w_up": gaussian(key_list[5], (EXPERTS, D, HID), D ** -0.5, 0.09375, ((0, 32),)),
        "w_down": gaussian(key_list[6], (EXPERTS, HID, D), HID ** -0.5, 0.1875, ((0, 32),)),
    }


def expert_apply(rows_in, gate_mat, up_mat, down_mat):
    gate_act = jnp.dot(rows_in, gate_mat, preferred_element_type=jnp.float32)
    up_act = jnp.dot(rows_in, up_mat, preferred_element_type=jnp.float32)
    hidden = (jax.nn.silu(gate_act) * up_act).astype(jnp.bfloat16)
    return jnp.dot(hidden, down_mat, preferred_element_type=jnp.float32).astype(jnp.bfloat16)


def reference(hidden_states, affinity, group_ids, expert_ids, w_gate, w_up, w_down):
    gate_weights = (2.5 * affinity / jnp.sum(affinity, axis=1, keepdims=True)).astype(jnp.bfloat16)
    pair_size = TOP_K // TOPG
    chosen = jnp.repeat(group_ids, pair_size, axis=1)
    is_valid = (expert_ids // EXP_GROUP) == chosen
    mixing = jnp.where(is_valid, gate_weights, jnp.zeros((), jnp.bfloat16))
    flat_ids = jnp.where(is_valid, expert_ids, -1).reshape(-1)
    flat_total = TOKENS * TOP_K
    capacity = EXPERTS * MOST

    def one_expert(collected, inputs):
        expert, gate_mat, up_mat, down_mat = inputs
        found_at = jnp.nonzero(flat_ids == expert, size=capacity, fill_value=flat_total)[0].astype(jnp.int32)
        token_rows = hidden_states[jnp.minimum(found_at, flat_total - 1) // TOP_K]
        produced = expert_apply(token_rows, gate_mat, up_mat, down_mat)
        return collected.at[found_at].set(produced, mode="drop"), None

    scanned = lax.scan(one_expert, jnp.zeros((flat_total, D), jnp.bfloat16),
                       (jnp.arange(EXPERTS, dtype=jnp.int32), w_gate, w_up, w_down))
    outputs = scanned[0]
    blocks = TOKENS // TOK_DEV
    outs_b = outputs.reshape(blocks, TOK_DEV, TOPG, pair_size, D)
    mix_b = mixing.reshape(blocks, TOK_DEV, TOPG, pair_size)

    def combine(inputs):
        block_out, block_mix = inputs
        group_part = jnp.einsum("tgk,tgkd->tgd", block_mix.astype(jnp.float32), block_out.astype(jnp.float32)).astype(jnp.bfloat16)
        group_part = lax.optimization_barrier(group_part)
        return jnp.sum(group_part.astype(jnp.float32), axis=1).astype(jnp.bfloat16)

    mixed_rows = lax.map(combine, (outs_b, mix_b))
    return mixed_rows.reshape(TOKENS, D)
```

```python
import functools

import jax
import jax.numpy as jnp
from jax import lax
from jax.experimental import pallas as pl
from jax.experimental.pallas import tpu as pltpu
from jax.sharding import PartitionSpec as P

ALL = ("row", "core", "plane", "column")
PLANE = ("row", "core", "column")
META = 16
OFFSET = 1 << 20
SMALL = 24 * 1024 * 1024
LARGE = 52 * 1024 * 1024


def plan(mesh_shape):
    group_count, local_count = mesh_shape["group"], mesh_shape["local"]
    cores = 2
    planes = 1
    while planes * planes < local_count:
        planes *= 2
    return group_count // cores, cores, planes, local_count // planes


def swap(value, axis, delta):
    size = lax.axis_size(axis)
    return lax.ppermute(value, axis, [(i, i ^ delta) for i in range(size)])


def swap_in_plane(value, dx, dy):
    xs, ys = lax.axis_size("column"), lax.axis_size("row")
    cs = lax.axis_size("core")
    pairs = [
        ((y * cs + c) * xs + x, ((y ^ dy) * cs + c) * xs + (x ^ dx))
        for y in range(ys)
        for c in range(cs)
        for x in range(xs)
    ]
    return lax.ppermute(value, PLANE, pairs)


def tile_of(width, most):
    best = 128
    for size in range(128, most + 1, 128):
        if width % size == 0:
            best = size
    return best


def call(
    kernel, grid, in_specs, out_specs, out_shape, scratch, flops, nbytes, after, operands, limit
):
    return pl.pallas_call(
        kernel,
        grid=grid,
        in_specs=list(in_specs) + [pl.BlockSpec(memory_space=pl.ANY)] * len(after),
        out_specs=out_specs,
        out_shape=out_shape,
        scratch_shapes=scratch,
        cost_estimate=pl.CostEstimate(flops=flops, bytes_accessed=nbytes, transcendentals=0),
        compiler_params=pltpu.CompilerParams(
            dimension_semantics=("arbitrary",), vmem_limit_bytes=limit
        ),
    )(*operands, *after)


def select_kernel(top_k, parts, n_after, want_ref, *refs):
    tokens = refs[:4]
    rest = refs[4 + n_after :]
    outs, (weight_ref, pick) = rest[:parts], rest[parts:]
    step = pl.program_id(0)
    tok = tokens[0].shape[0] - META

    @pl.when(step == 0)
    def _():
        want = want_ref[...]
        rows_all = want.shape[0]
        for at, ref in enumerate(tokens[::2]):
            info = ref[tok : tok + META, : 3 * tok].astype(jnp.float32)
            code = info[:, :tok] * tok + info[:, tok : 2 * tok] + float(at * OFFSET)
            found = jnp.zeros((rows_all, tok), jnp.float32)
            weight = jnp.zeros((rows_all, tok), jnp.float32)
            for k in range(top_k):
                hit = code[k : k + 1, :] == want
                found = jnp.where(hit, 1.0, found)
                weight = jnp.where(hit, info[k : k + 1, 2 * tok :], weight)
            pick[:, at * tok : (at + 1) * tok] = found.astype(jnp.bfloat16)
            weight_ref[at * tok : (at + 1) * tok, :] = weight.T.astype(jnp.bfloat16)

    for half in range(2):

        @pl.when(step == half)
        def _():
            own, sib = tokens[half][:tok, :], tokens[2 + half][:tok, :]
            rows = jnp.dot(pick[:, :tok], own, preferred_element_type=jnp.float32)
            rows += jnp.dot(pick[:, tok:], sib, preferred_element_type=jnp.float32)
            rows = rows.astype(jnp.bfloat16)
            pair = outs[0].shape[0]
            for i, out in enumerate(outs):
                out[...] = rows[i * pair : (i + 1) * pair]


def select(want, own, sib, top_k, parts, after):
    rows_all = want.shape[0]
    tok, tile = own[0].shape[0] - META, own[0].shape[1]
    width = 2 * tile
    pair = rows_all // parts
    kernel = functools.partial(select_kernel, top_k, parts, len(after))
    *sent, weight = call(
        kernel,
        (2,),
        [pl.BlockSpec((rows_all, 1), lambda j: (0, 0))]
        + [pl.BlockSpec((tok + META, tile), lambda j: (0, 0))] * 4,
        [pl.BlockSpec((pair, tile), lambda j: (0, j))] * parts
        + [pl.BlockSpec((2 * tok, rows_all), lambda j: (0, 0))],
        [jax.ShapeDtypeStruct((pair, width), jnp.bfloat16)] * parts
        + [jax.ShapeDtypeStruct((2 * tok, rows_all), jnp.bfloat16)],
        [pltpu.VMEM((rows_all, 2 * tok), jnp.bfloat16)],
        4 * rows_all * tok * width,
        2 * width * (2 * tok + rows_all),
        after,
        (want, *own, *sib),
        SMALL,
    )
    return sent, weight


def expert_kernel(parts, first, n_after, *refs):
    rows, (gate_ref, up_ref, down_ref) = refs[:parts], refs[parts : parts + 3]
    rest = refs[parts + 3 + n_after :]
    outs, (rows_in, hidden) = rest[:parts], rest[parts:]
    step = pl.program_id(0)
    pair = rows[0].shape[0]
    tile = gate_ref.shape[2]

    @pl.when(step == 0)
    def _():
        for i in range(parts):
            rows_in[pl.ds(i * pair, pair), :] = rows[i][...]

    @pl.when(step < first)
    def _():
        data = rows_in[...]
        gate_act = jnp.dot(data, gate_ref[0], preferred_element_type=jnp.float32)
        up_act = jnp.dot(data, up_ref[0], preferred_element_type=jnp.float32)
        act = gate_act / (1.0 + jnp.exp(-gate_act)) * up_act
        for i in range(first):

            @pl.when(step == i)
            def _():
                hidden[:, i * tile : (i + 1) * tile] = act.astype(jnp.bfloat16)

    @pl.when(step >= first)
    def _():
        made = jnp.dot(hidden[...], down_ref[0], preferred_element_type=jnp.float32)
        made = made.astype(jnp.bfloat16)
        for i in range(parts):
            outs[i][...] = made[i * pair : (i + 1) * pair]


def expert(rows, w_gate, w_up, w_down, after):
    parts = len(rows)
    pair, width = rows[0].shape
    hid = w_gate.shape[2]
    tile_h, tile_w = tile_of(hid, 256), tile_of(width, 512)
    first = hid // tile_h
    second = width // tile_w
    kernel = functools.partial(expert_kernel, parts, first, len(after))

    def early(j):
        return (0, 0, jnp.minimum(j, first - 1))

    def late(j):
        return (0, 0, jnp.maximum(j - first, 0))

    return call(
        kernel,
        (first + second,),
        [pl.BlockSpec((pair, width), lambda j: (0, 0))] * parts
        + [
            pl.BlockSpec((1, width, tile_h), early),
            pl.BlockSpec((1, width, tile_h), early),
            pl.BlockSpec((1, hid, tile_w), late),
        ],
        [pl.BlockSpec((pair, tile_w), lambda j: (0, jnp.maximum(j - first, 0)))] * parts,
        [jax.ShapeDtypeStruct((pair, width), jnp.bfloat16)] * parts,
        [
            pltpu.VMEM((parts * pair, width), jnp.bfloat16),
            pltpu.VMEM((parts * pair, hid), jnp.bfloat16),
        ],
        6 * parts * pair * hid * width,
        6 * hid * width + 4 * parts * pair * width,
        after,
        (*rows, w_gate, w_up, w_down),
        LARGE,
    )


def combine_kernel(parts, n_after, weight_ref, *refs):
    home = refs[:parts]
    own_ref, left_ref, right_ref, rows = refs[parts + n_after :]
    step = pl.program_id(0)
    tok = own_ref.shape[0]
    pair = home[0].shape[0]
    for i in range(parts):
        rows[pl.ds(i * pair, pair), :] = home[i][...]
    mixed = jnp.dot(weight_ref[...], rows[...], preferred_element_type=jnp.float32)
    own_ref[...] = mixed[:tok]
    for half, sib_ref in enumerate((left_ref, right_ref)):

        @pl.when(step == half)
        def _():
            sib_ref[...] = mixed[tok:].astype(jnp.bfloat16)


def combine(weight, home, after):
    parts = len(home)
    both, rows_all = weight.shape
    tok = both // 2
    pair, width = home[0].shape
    tile = width // 2
    half = pl.BlockSpec((tok, tile), lambda j: (0, 0))
    return call(
        functools.partial(combine_kernel, parts, len(after)),
        (2,),
        [pl.BlockSpec((both, rows_all), lambda j: (0, 0))]
        + [pl.BlockSpec((pair, tile), lambda j: (0, j))] * parts,
        [pl.BlockSpec((tok, tile), lambda j: (0, j)), half, half],
        [jax.ShapeDtypeStruct((tok, width), jnp.float32)]
        + [jax.ShapeDtypeStruct((tok, tile), jnp.bfloat16)] * 2,
        [pltpu.VMEM((rows_all, tile), jnp.bfloat16)],
        2 * rows_all * both * width,
        2 * width * (both * 2 + rows_all),
        after,
        (weight, *home),
        SMALL,
    )


def pass_kernel(count, n_after, *refs):
    outs = refs[count + n_after :]
    for i in range(count):
        outs[i][...] = refs[i][...]


def passed(values, after):
    rows, width = values[0].shape
    tile = tile_of(width, width // 2)
    count = len(values)
    return call(
        functools.partial(pass_kernel, count, len(after)),
        (width // tile,),
        [pl.BlockSpec((rows, tile), lambda j: (0, j))] * count,
        [pl.BlockSpec((rows, tile), lambda j: (0, j))] * count,
        [jax.ShapeDtypeStruct(value.shape, value.dtype) for value in values],
        [],
        1,
        4 * count * rows * width,
        after,
        tuple(values),
        SMALL,
    )


def relay_kernel(chooser, copies, whole, count, n_after, plane_ref, *refs):
    step = pl.program_id(0)
    values = [ref[...] for ref in refs[:count]]
    left_ref, right_ref, *outs = refs[count + n_after :]
    kept = chooser(plane_ref[0], *values)
    for half, ref in enumerate((left_ref, right_ref)):

        @pl.when(step == half)
        def _():
            ref[...] = kept

    for value, out in zip([kept] * whole + values[:copies], outs):
        out[...] = value


def relay(chooser, plane, values, whole, copies, after):
    rows, width = values[0].shape
    tile = width // 2
    count = len(values)
    block = pl.BlockSpec((rows, tile), lambda j: (0, j))
    half = pl.BlockSpec((rows, tile), lambda j: (0, 0))
    return call(
        functools.partial(relay_kernel, chooser, copies, whole, count, len(after)),
        (2,),
        [pl.BlockSpec(memory_space=pltpu.SMEM)] + [block] * count,
        [half, half] + [block] * (whole + copies),
        [jax.ShapeDtypeStruct((rows, tile), jnp.bfloat16)] * 2
        + [jax.ShapeDtypeStruct((rows, width), jnp.bfloat16)] * (whole + copies),
        [],
        1,
        2 * (count + 1 + whole + copies) * rows * width,
        after,
        (plane, *values),
        SMALL,
    )


def add_kernel(n_after, own_ref, left_ref, right_ref, *rest):
    out_ref = rest[n_after]
    half = left_ref.shape[1]
    for at, ref in enumerate((left_ref, right_ref)):
        part = own_ref[:, at * half : (at + 1) * half] + ref[...].astype(jnp.float32)
        out_ref[:, at * half : (at + 1) * half] = part.astype(out_ref.dtype)


def added(own, sib, after):
    tok, width = own.shape
    half = pl.BlockSpec((tok, width // 2), lambda j: (0, 0))
    whole = pl.BlockSpec((tok, width), lambda j: (0, 0))
    return call(
        functools.partial(add_kernel, len(after)),
        (1,),
        [whole, half, half],
        whole,
        jax.ShapeDtypeStruct((tok, width), jnp.bfloat16),
        [],
        tok * width,
        8 * tok * width,
        after,
        (own, *sib),
        SMALL,
    )


def route(affinity, group_ids, expert_ids, experts_all, local_count):
    tok_rows, top_k = expert_ids.shape
    pair_size = top_k // group_ids.shape[1]
    gate_weights = (2.5 * affinity / jnp.sum(affinity, axis=1, keepdims=True)).astype(jnp.bfloat16)
    chosen = jnp.repeat(group_ids, pair_size, axis=1)
    is_valid = expert_ids // local_count == chosen
    mixing = jnp.where(is_valid, gate_weights, jnp.zeros((), jnp.bfloat16)).T
    target = jnp.where(is_valid, expert_ids, -1).T
    is_member = target[:, None, :] == jnp.arange(experts_all)[None, :, None]
    member = jnp.sum(is_member.astype(jnp.float32), axis=0).astype(jnp.bfloat16)
    earlier = (jnp.arange(tok_rows)[:, None] < jnp.arange(tok_rows)[None, :]).astype(jnp.bfloat16)
    before = jnp.dot(member, earlier, preferred_element_type=jnp.float32)
    slot = jnp.sum(jnp.where(is_member, before[None], 0.0), axis=1)
    info = [target.astype(jnp.bfloat16), slot.astype(jnp.bfloat16), mixing]
    return jnp.pad(jnp.concatenate(info, axis=1), ((0, META - top_k), (0, 0)))


def shards(dims, hidden_states, affinity, group_ids, expert_ids, w_gate, w_up, w_down):
    ys, cs, zs, xs = dims
    tok_rows, width = hidden_states.shape
    top_k = expert_ids.shape[1]
    local_count = zs * xs
    experts_all = ys * cs * local_count
    most_rows = 5 * tok_rows * top_k // (4 * experts_all)
    me_y, me_c = lax.axis_index("row"), lax.axis_index("core")
    me_z, me_x = lax.axis_index("plane"), lax.axis_index("column")
    plane = me_z.astype(jnp.int32).reshape(1)

    meta = route(affinity, group_ids, expert_ids, experts_all, local_count)
    meta = jnp.pad(meta, ((0, 0), (0, width - meta.shape[1])))
    payload = jnp.concatenate([hidden_states, meta], axis=0)
    middle = width // 2
    payload_halves = [
        jnp.concatenate([hidden_states[:, :middle], meta[:, :middle]], axis=0),
        jnp.concatenate([hidden_states[:, middle:], meta[:, middle:]], axis=0),
    ]

    rel = [(dx, dy) for dx in range(xs) for dy in range(ys)]
    parts = len(rel)
    pair = -(-cs * most_rows // 16) * 16
    wanted = jnp.stack(
        [((me_y ^ dy) * cs + me_c) * local_count + me_z * xs + (me_x ^ dx) for dx, dy in rel]
    ).astype(jnp.float32)
    row = jnp.arange(pair)
    in_pair = jnp.where(
        row < cs * most_rows, row // most_rows * OFFSET + row % most_rows, -2 * OFFSET
    ).astype(jnp.float32)
    want = (wanted[:, None] * tok_rows + in_pair[None, :]).reshape(-1, 1)

    tokens, siblings, arrived, weights, made, halves, sums = {}, {}, {}, {}, {}, {}, {}
    last = []

    def hop(value, step, sources):
        return lax.ppermute(value, "plane", [(z, z + step) for z in sources])

    def have(dz, halves):
        tokens[dz] = halves
        siblings[dz] = [swap(half, "core", 1) for half in halves]

    def relayed(dz, chooser, values, whole, copies, *after):
        left, right, *outs = relay(chooser, plane, values, whole, copies, last + list(after))
        last[:] = [left]
        have(dz, (left, right))
        return outs

    def in_plane(values):
        return [
            part if (dx, dy) == (0, 0) else swap_in_plane(part, dx, dy)
            for part, (dx, dy) in zip(values, rel)
        ]

    def dispatch(dz, *after):
        sent, weights[dz] = select(
            want, tokens[dz], siblings[dz], top_k, parts, last + list(after)
        )
        last[:] = [weights[dz]]
        arrived[dz] = in_plane(sent)

    def apply(dz, *after):
        made[dz] = expert(arrived[dz], w_gate, w_up, w_down, last + list(after))
        last[:] = [made[dz][0]]

    def give_back(dz, late=False):
        sent = made[dz]
        if late:
            sent = passed(sent, last)
            last[:] = [sent[0]]
        halves[dz] = in_plane(sent)

    def collect(dz, *after):
        own, *sib = combine(weights[dz], halves[dz], last + list(after))
        last[:] = [sib[0]]
        halves[dz] = own, [swap(half, "core", 1) for half in sib]

    def send_home(dz, *after):
        part = added(*halves[dz], last + list(after))
        last[:] = [part]
        sums[dz] = swap(part, "plane", dz)

    up1, down1 = hop(payload, 1, (0, 1, 2)), hop(payload, -1, (1, 2, 3))
    have(0, payload_halves)
    dispatch(0)
    up1, down1 = relayed(
        1, lambda z, u, d: jnp.where(z % 2 == 1, u, d), [up1, down1], 0, 2, *arrived[0]
    )
    up2, down2 = hop(up1, 1, (1, 2)), hop(down1, -1, (1, 2))
    dispatch(1)
    apply(0)
    (second,) = relayed(
        2, lambda z, u, d: jnp.where(z >= 2, u, d), [up2, down2], 1, 0, *arrived[1]
    )
    ends = lax.ppermute(second, "plane", [(1, 0), (2, 3)])
    dispatch(2)
    apply(1)
    relayed(
        3,
        lambda z, u, d, e: jnp.where(z == 1, d, jnp.where(z == 2, u, e)),
        [up1, down1, ends],
        0,
        0,
        *arrived[2],
    )
    dispatch(3)
    apply(2)
    give_back(2)
    apply(3)
    give_back(3)
    collect(2)
    send_home(2)
    give_back(1, late=True)
    collect(3)
    send_home(3, sums[2])
    give_back(0, late=True)
    collect(1)
    send_home(1, sums[3])
    collect(0)
    own, sib = halves[0]
    sums[0] = own + jnp.concatenate(sib, axis=1).astype(jnp.float32)
    total = sums[0]
    for dz in range(1, zs):
        total = total + sums[dz].astype(jnp.float32)
    return total.astype(jnp.bfloat16)


def solution(mesh):
    dims = plan(mesh.shape)
    finer = jax.sharding.Mesh(mesh.devices.reshape(dims), ALL)

    def body(*args):
        return shards(dims, *args)

    placed = (P(ALL, None),) * 4 + (P(ALL, None, None),) * 3
    return jax.shard_map(body, mesh=finer, in_specs=placed, out_specs=P(ALL, None), check_vma=False)
```

```python
import functools

import jax
import jax.numpy as jnp
from jax import lax
from jax.experimental import pallas as pl
from jax.experimental.pallas import tpu as pltpu
from jax.sharding import PartitionSpec as P

ALL = ("row", "core", "plane", "column")
PLANE = ("row", "core", "column")
META = 16
OFFSET = 1 << 20
SMALL = 24 * 1024 * 1024
LARGE = 52 * 1024 * 1024


def plan(mesh_shape):
    group_count, local_count = mesh_shape["group"], mesh_shape["local"]
    cores = 2
    planes = 1
    while planes * planes < local_count:
        planes *= 2
    return group_count // cores, cores, planes, local_count // planes


def swap(value, axis, delta):
    size = lax.axis_size(axis)
    return lax.ppermute(value, axis, [(i, i ^ delta) for i in range(size)])


def swap_in_plane(value, dx, dy):
    xs, ys = lax.axis_size("column"), lax.axis_size("row")
    cs = lax.axis_size("core")
    pairs = [
        ((y * cs + c) * xs + x, ((y ^ dy) * cs + c) * xs + (x ^ dx))
        for y in range(ys)
        for c in range(cs)
        for x in range(xs)
    ]
    return lax.ppermute(value, PLANE, pairs)


def tile_of(width, most):
    best = 128
    for size in range(128, most + 1, 128):
        if width % size == 0:
            best = size
    return best


def call(
    kernel, grid, in_specs, out_specs, out_shape, scratch, flops, nbytes, after, operands, limit
):
    return pl.pallas_call(
        kernel,
        grid=grid,
        in_specs=list(in_specs) + [pl.BlockSpec(memory_space=pl.ANY)] * len(after),
        out_specs=out_specs,
        out_shape=out_shape,
        scratch_shapes=scratch,
        cost_estimate=pl.CostEstimate(flops=1, bytes_accessed=1, transcendentals=0),
        compiler_params=pltpu.CompilerParams(
            dimension_semantics=("arbitrary",), vmem_limit_bytes=limit
        ),
    )(*operands, *after)


def select_kernel(top_k, parts, n_after, want_ref, *refs):
    tokens = refs[:4]
    rest = refs[4 + n_after :]
    outs, (weight_ref, pick) = rest[:parts], rest[parts:]
    step = pl.program_id(0)
    tok = tokens[0].shape[0] - META

    @pl.when(step == 0)
    def _():
        want = want_ref[...]
        rows_all = want.shape[0]
        for at, ref in enumerate(tokens[::2]):
            info = ref[tok : tok + META, : 3 * tok].astype(jnp.float32)
            code = info[:, :tok] * tok + info[:, tok : 2 * tok] + float(at * OFFSET)
            found = jnp.zeros((rows_all, tok), jnp.float32)
            weight = jnp.zeros((rows_all, tok), jnp.float32)
            for k in range(top_k):
                hit = code[k : k + 1, :] == want
                found = jnp.where(hit, 1.0, found)
                weight = jnp.where(hit, info[k : k + 1, 2 * tok :], weight)
            pick[:, at * tok : (at + 1) * tok] = found.astype(jnp.bfloat16)
            weight_ref[at * tok : (at + 1) * tok, :] = weight.T.astype(jnp.bfloat16)

    for half in range(2):

        @pl.when(step == half)
        def _():
            own, sib = tokens[half][:tok, :], tokens[2 + half][:tok, :]
            rows = jnp.dot(pick[:, :tok], own, preferred_element_type=jnp.float32)
            rows += jnp.dot(pick[:, tok:], sib, preferred_element_type=jnp.float32)
            rows = rows.astype(jnp.bfloat16)
            pair = outs[0].shape[0]
            for i, out in enumerate(outs):
                out[...] = rows[i * pair : (i + 1) * pair]


def select(want, own, sib, top_k, parts, after):
    rows_all = want.shape[0]
    tok, tile = own[0].shape[0] - META, own[0].shape[1]
    width = 2 * tile
    pair = rows_all // parts
    kernel = functools.partial(select_kernel, top_k, parts, len(after))
    *sent, weight = call(
        kernel,
        (2,),
        [pl.BlockSpec((rows_all, 1), lambda j: (0, 0))]
        + [pl.BlockSpec((tok + META, tile), lambda j: (0, 0))] * 4,
        [pl.BlockSpec((pair, tile), lambda j: (0, j))] * parts
        + [pl.BlockSpec((2 * tok, rows_all), lambda j: (0, 0))],
        [jax.ShapeDtypeStruct((pair, width), jnp.bfloat16)] * parts
        + [jax.ShapeDtypeStruct((2 * tok, rows_all), jnp.bfloat16)],
        [pltpu.VMEM((rows_all, 2 * tok), jnp.bfloat16)],
        4 * rows_all * tok * width,
        2 * width * (2 * tok + rows_all),
        after,
        (want, *own, *sib),
        SMALL,
    )
    return sent, weight


def expert_kernel(parts, first, n_after, *refs):
    rows, (gate_ref, up_ref, down_ref) = refs[:parts], refs[parts : parts + 3]
    rest = refs[parts + 3 + n_after :]
    outs, (rows_in, hidden) = rest[:parts], rest[parts:]
    step = pl.program_id(0)
    pair = rows[0].shape[0]
    tile = gate_ref.shape[2]

    @pl.when(step == 0)
    def _():
        for i in range(parts):
            rows_in[pl.ds(i * pair, pair), :] = rows[i][...]

    @pl.when(step < first)
    def _():
        data = rows_in[...]
        gate_act = jnp.dot(data, gate_ref[0], preferred_element_type=jnp.float32)
        up_act = jnp.dot(data, up_ref[0], preferred_element_type=jnp.float32)
        act = gate_act / (1.0 + jnp.exp(-gate_act)) * up_act
        for i in range(first):

            @pl.when(step == i)
            def _():
                hidden[:, i * tile : (i + 1) * tile] = act.astype(jnp.bfloat16)

    @pl.when(step >= first)
    def _():
        made = jnp.dot(hidden[...], down_ref[0], preferred_element_type=jnp.float32)
        made = made.astype(jnp.bfloat16)
        for i in range(parts):
            outs[i][...] = made[i * pair : (i + 1) * pair]


def expert(rows, w_gate, w_up, w_down, after):
    parts = len(rows)
    pair, width = rows[0].shape
    hid = w_gate.shape[2]
    tile_h, tile_w = tile_of(hid, 256), tile_of(width, 512)
    first = hid // tile_h
    second = width // tile_w
    kernel = functools.partial(expert_kernel, parts, first, len(after))

    def early(j):
        return (0, 0, jnp.minimum(j, first - 1))

    def late(j):
        return (0, 0, jnp.maximum(j - first, 0))

    return call(
        kernel,
        (first + second,),
        [pl.BlockSpec((pair, width), lambda j: (0, 0))] * parts
        + [
            pl.BlockSpec((1, width, tile_h), early),
            pl.BlockSpec((1, width, tile_h), early),
            pl.BlockSpec((1, hid, tile_w), late),
        ],
        [pl.BlockSpec((pair, tile_w), lambda j: (0, jnp.maximum(j - first, 0)))] * parts,
        [jax.ShapeDtypeStruct((pair, width), jnp.bfloat16)] * parts,
        [
            pltpu.VMEM((parts * pair, width), jnp.bfloat16),
            pltpu.VMEM((parts * pair, hid), jnp.bfloat16),
        ],
        6 * parts * pair * hid * width,
        6 * hid * width + 4 * parts * pair * width,
        after,
        (*rows, w_gate, w_up, w_down),
        LARGE,
    )


def combine_kernel(parts, n_after, weight_ref, *refs):
    home = refs[:parts]
    own_ref, left_ref, right_ref, rows = refs[parts + n_after :]
    step = pl.program_id(0)
    tok = own_ref.shape[0]
    pair = home[0].shape[0]
    for i in range(parts):
        rows[pl.ds(i * pair, pair), :] = home[i][...]
    mixed = jnp.dot(weight_ref[...], rows[...], preferred_element_type=jnp.float32)
    own_ref[...] = mixed[:tok]
    for half, sib_ref in enumerate((left_ref, right_ref)):

        @pl.when(step == half)
        def _():
            sib_ref[...] = mixed[tok:].astype(jnp.bfloat16)


def combine(weight, home, after):
    parts = len(home)
    both, rows_all = weight.shape
    tok = both // 2
    pair, width = home[0].shape
    tile = width // 2
    half = pl.BlockSpec((tok, tile), lambda j: (0, 0))
    return call(
        functools.partial(combine_kernel, parts, len(after)),
        (2,),
        [pl.BlockSpec((both, rows_all), lambda j: (0, 0))]
        + [pl.BlockSpec((pair, tile), lambda j: (0, j))] * parts,
        [pl.BlockSpec((tok, tile), lambda j: (0, j)), half, half],
        [jax.ShapeDtypeStruct((tok, width), jnp.float32)]
        + [jax.ShapeDtypeStruct((tok, tile), jnp.bfloat16)] * 2,
        [pltpu.VMEM((rows_all, tile), jnp.bfloat16)],
        2 * rows_all * both * width,
        2 * width * (both * 2 + rows_all),
        after,
        (weight, *home),
        SMALL,
    )


def pass_kernel(count, n_after, *refs):
    outs = refs[count + n_after :]
    for i in range(count):
        outs[i][...] = refs[i][...]


def passed(values, after):
    rows, width = values[0].shape
    tile = tile_of(width, width // 2)
    count = len(values)
    return call(
        functools.partial(pass_kernel, count, len(after)),
        (width // tile,),
        [pl.BlockSpec((rows, tile), lambda j: (0, j))] * count,
        [pl.BlockSpec((rows, tile), lambda j: (0, j))] * count,
        [jax.ShapeDtypeStruct(value.shape, value.dtype) for value in values],
        [],
        1,
        4 * count * rows * width,
        after,
        tuple(values),
        SMALL,
    )


def relay_kernel(chooser, copies, whole, count, n_after, plane_ref, *refs):
    step = pl.program_id(0)
    values = [ref[...] for ref in refs[:count]]
    left_ref, right_ref, *outs = refs[count + n_after :]
    kept = chooser(plane_ref[0], *values)
    for half, ref in enumerate((left_ref, right_ref)):

        @pl.when(step == half)
        def _():
            ref[...] = kept

    for value, out in zip([kept] * whole + values[:copies], outs):
        out[...] = value


def relay(chooser, plane, values, whole, copies, after):
    rows, width = values[0].shape
    tile = width // 2
    count = len(values)
    block = pl.BlockSpec((rows, tile), lambda j: (0, j))
    half = pl.BlockSpec((rows, tile), lambda j: (0, 0))
    return call(
        functools.partial(relay_kernel, chooser, copies, whole, count, len(after)),
        (2,),
        [pl.BlockSpec(memory_space=pltpu.SMEM)] + [block] * count,
        [half, half] + [block] * (whole + copies),
        [jax.ShapeDtypeStruct((rows, tile), jnp.bfloat16)] * 2
        + [jax.ShapeDtypeStruct((rows, width), jnp.bfloat16)] * (whole + copies),
        [],
        1,
        2 * (count + 1 + whole + copies) * rows * width,
        after,
        (plane, *values),
        SMALL,
    )


def add_kernel(n_after, own_ref, left_ref, right_ref, *rest):
    out_ref = rest[n_after]
    tok, half = left_ref.shape
    for at, ref in enumerate((left_ref, right_ref)):
        part = own_ref[:, at * half : (at + 1) * half] + ref[...].astype(jnp.float32)
        out_ref[:tok, at * half : (at + 1) * half] = part.astype(out_ref.dtype)
    if out_ref.shape[0] > tok:
        rest_of = out_ref.shape[0] - tok
        out_ref[tok:, :] = jnp.zeros((rest_of, 2 * half), out_ref.dtype)


def added(own, sib, after, extra=0):
    tok, width = own.shape
    half = pl.BlockSpec((tok, width // 2), lambda j: (0, 0))
    whole = pl.BlockSpec((tok, width), lambda j: (0, 0))
    return call(
        functools.partial(add_kernel, len(after)),
        (1,),
        [whole, half, half],
        pl.BlockSpec((tok + extra, width), lambda j: (0, 0)),
        jax.ShapeDtypeStruct((tok + extra, width), jnp.bfloat16),
        [],
        tok * width,
        8 * tok * width,
        after,
        (own, *sib),
        SMALL,
    )


def route(affinity, group_ids, expert_ids, experts_all, local_count):
    tok_rows, top_k = expert_ids.shape
    pair_size = top_k // group_ids.shape[1]
    gate_weights = (2.5 * affinity / jnp.sum(affinity, axis=1, keepdims=True)).astype(jnp.bfloat16)
    chosen = jnp.repeat(group_ids, pair_size, axis=1)
    is_valid = expert_ids // local_count == chosen
    mixing = jnp.where(is_valid, gate_weights, jnp.zeros((), jnp.bfloat16)).T
    target = jnp.where(is_valid, expert_ids, -1).T
    is_member = target[:, None, :] == jnp.arange(experts_all)[None, :, None]
    member = jnp.sum(is_member.astype(jnp.float32), axis=0).astype(jnp.bfloat16)
    earlier = (jnp.arange(tok_rows)[:, None] < jnp.arange(tok_rows)[None, :]).astype(jnp.bfloat16)
    before = jnp.dot(member, earlier, preferred_element_type=jnp.float32)
    slot = jnp.sum(jnp.where(is_member, before[None], 0.0), axis=1)
    info = [target.astype(jnp.bfloat16), slot.astype(jnp.bfloat16), mixing]
    return jnp.pad(jnp.concatenate(info, axis=1), ((0, META - top_k), (0, 0)))


def shards(dims, hidden_states, affinity, group_ids, expert_ids, w_gate, w_up, w_down):
    ys, cs, zs, xs = dims
    tok_rows, width = hidden_states.shape
    top_k = expert_ids.shape[1]
    local_count = zs * xs
    experts_all = ys * cs * local_count
    most_rows = 5 * tok_rows * top_k // (4 * experts_all)
    me_y, me_c = lax.axis_index("row"), lax.axis_index("core")
    me_z, me_x = lax.axis_index("plane"), lax.axis_index("column")
    plane = me_z.astype(jnp.int32).reshape(1)

    meta = route(affinity, group_ids, expert_ids, experts_all, local_count)
    meta = jnp.pad(meta, ((0, 0), (0, width - meta.shape[1])))
    payload = jnp.concatenate([hidden_states, meta], axis=0)
    middle = width // 2
    payload_halves = [
        jnp.concatenate([hidden_states[:, :middle], meta[:, :middle]], axis=0),
        jnp.concatenate([hidden_states[:, middle:], meta[:, middle:]], axis=0),
    ]

    rel = [(dx, dy) for dx in range(xs) for dy in range(ys)]
    parts = len(rel)
    pair = -(-cs * most_rows // 16) * 16
    wanted = jnp.stack(
        [((me_y ^ dy) * cs + me_c) * local_count + me_z * xs + (me_x ^ dx) for dx, dy in rel]
    ).astype(jnp.float32)
    row = jnp.arange(pair)
    in_pair = jnp.where(
        row < cs * most_rows, row // most_rows * OFFSET + row % most_rows, -2 * OFFSET
    ).astype(jnp.float32)
    want = (wanted[:, None] * tok_rows + in_pair[None, :]).reshape(-1, 1)

    tokens, siblings, arrived, weights, made, halves, sums = {}, {}, {}, {}, {}, {}, {}
    last = []

    def hop(value, step, sources):
        return lax.ppermute(value, "plane", [(z, z + step) for z in sources])

    def have(dz, halves):
        tokens[dz] = halves
        siblings[dz] = [swap(half, "core", 1) for half in halves]

    def relayed(dz, chooser, values, whole, copies, *after):
        left, right, *outs = relay(chooser, plane, values, whole, copies, last + list(after))
        last[:] = [left]
        have(dz, (left, right))
        return outs

    def in_plane(values):
        return [
            part if (dx, dy) == (0, 0) else swap_in_plane(part, dx, dy)
            for part, (dx, dy) in zip(values, rel)
        ]

    def send_free(dz):
        own, sib = halves[dz]
        part = own + jnp.concatenate(sib, axis=1).astype(jnp.float32)
        sums[dz] = swap(part.astype(jnp.bfloat16), "plane", dz)

    def tick(*after):
        (out,) = passed([meta[:, : 3 * tok_rows]], last + list(after))
        last[:] = [out]

    def dispatch(dz, *after):
        sent, weights[dz] = select(
            want, tokens[dz], siblings[dz], top_k, parts, last + list(after)
        )
        last[:] = [weights[dz]]
        arrived[dz] = in_plane(sent)

    def apply(dz, *after):
        made[dz] = expert(arrived[dz], w_gate, w_up, w_down, last + list(after))
        last[:] = [made[dz][0]]

    def give_back(dz, late=False):
        sent = made[dz]
        if late:
            sent = passed(sent, last)
            last[:] = [sent[0]]
        halves[dz] = in_plane(sent)

    def collect(dz, *after, whole=False):
        own, *sib = combine(weights[dz], halves[dz], last + list(after))
        last[:] = [sib[0]]
        if whole:
            came = swap(jnp.concatenate(sib, axis=1), "core", 1)
            halves[dz] = own, [came[:, :middle], came[:, middle:]]
            return
        halves[dz] = own, [swap(half, "core", 1) for half in sib]

    def send_home(dz, *after, extra=0):
        part = added(*halves[dz], last + list(after), extra)
        last[:] = [part]
        sums[dz] = swap(part, "plane", dz)

    up1, down1 = hop(payload, 1, (0, 1, 2)), hop(payload, -1, (1, 2, 3))
    have(0, payload_halves)
    dispatch(0)
    up1, down1 = relayed(
        1, lambda z, u, d: jnp.where(z % 2 == 1, u, d), [up1, down1], 0, 2, *arrived[0]
    )
    up2, down2 = hop(up1, 1, (1, 2)), hop(down1, -1, (1, 2))
    dispatch(1)
    apply(0)
    (second,) = relayed(
        2, lambda z, u, d: jnp.where(z >= 2, u, d), [up2, down2], 1, 0, *arrived[1]
    )
    ends = lax.ppermute(second, "plane", [(1, 0), (2, 3)])
    dispatch(2)
    apply(1)
    relayed(
        3,
        lambda z, u, d, e: jnp.where(z == 1, d, jnp.where(z == 2, u, e)),
        [up1, down1, ends],
        0,
        0,
    )
    dispatch(3, *arrived[2])
    apply(2)
    give_back(2)
    apply(3)
    give_back(3)
    collect(2)
    send_home(2)
    give_back(1, late=True)
    collect(3, whole=True)
    tick(sums[2])
    send_home(3)
    give_back(0, late=True)
    collect(1)
    send_free(1)
    tick(sums[3])
    collect(0)
    own, sib = halves[0]
    sums[0] = own + jnp.concatenate(sib, axis=1).astype(jnp.float32)
    total = sums[0]
    for dz in range(1, zs):
        total = total + sums[dz][:tok_rows].astype(jnp.float32)
    return total.astype(jnp.bfloat16)


def solution(mesh):
    dims = plan(mesh.shape)
    finer = jax.sharding.Mesh(mesh.devices.reshape(dims), ALL)

    def body(*args):
        return shards(dims, *args)

    placed = (P(ALL, None),) * 4 + (P(ALL, None, None),) * 3
    return jax.shard_map(body, mesh=finer, in_specs=placed, out_specs=P(ALL, None), check_vma=False)
```

```python
import functools

import jax
import jax.numpy as jnp
from jax import lax
from jax.experimental import pallas as pl
from jax.experimental.pallas import tpu as pltpu
from jax.sharding import PartitionSpec as P

ALL = ("row", "core", "plane", "column")
PLANE = ("row", "core", "column")
META = 16
OFFSET = 1 << 20
SMALL = 24 * 1024 * 1024
LARGE = 52 * 1024 * 1024


def plan(mesh_shape):
    group_count, local_count = mesh_shape["group"], mesh_shape["local"]
    cores = 2
    planes = 1
    while planes * planes < local_count:
        planes *= 2
    return group_count // cores, cores, planes, local_count // planes


def swap(value, axis, delta):
    size = lax.axis_size(axis)
    return lax.ppermute(value, axis, [(i, i ^ delta) for i in range(size)])


def swap_in_plane(value, dx, dy):
    xs, ys = lax.axis_size("column"), lax.axis_size("row")
    cs = lax.axis_size("core")
    pairs = [
        ((y * cs + c) * xs + x, ((y ^ dy) * cs + c) * xs + (x ^ dx))
        for y in range(ys)
        for c in range(cs)
        for x in range(xs)
    ]
    return lax.ppermute(value, PLANE, pairs)


def tile_of(width, most):
    best = 128
    for size in range(128, most + 1, 128):
        if width % size == 0:
            best = size
    return best


def call(
    kernel, grid, in_specs, out_specs, out_shape, scratch, flops, nbytes, after, operands, limit
):
    return pl.pallas_call(
        kernel,
        grid=grid,
        in_specs=list(in_specs) + [pl.BlockSpec(memory_space=pl.ANY)] * len(after),
        out_specs=out_specs,
        out_shape=out_shape,
        scratch_shapes=scratch,
        cost_estimate=pl.CostEstimate(flops=flops, bytes_accessed=nbytes, transcendentals=0),
        compiler_params=pltpu.CompilerParams(
            dimension_semantics=("arbitrary",), vmem_limit_bytes=limit
        ),
    )(*operands, *after)


def select_kernel(top_k, parts, n_after, want_ref, *refs):
    tokens = refs[:4]
    rest = refs[4 + n_after :]
    outs, (weight_ref, pick) = rest[:parts], rest[parts:]
    step = pl.program_id(0)
    tok = tokens[0].shape[0] - META

    @pl.when(step == 0)
    def _():
        want = want_ref[...]
        rows_all = want.shape[0]
        for at, ref in enumerate(tokens[::2]):
            info = ref[tok : tok + META, : 3 * tok].astype(jnp.float32)
            code = info[:, :tok] * tok + info[:, tok : 2 * tok] + float(at * OFFSET)
            found = jnp.zeros((rows_all, tok), jnp.float32)
            weight = jnp.zeros((rows_all, tok), jnp.float32)
            for k in range(top_k):
                hit = code[k : k + 1, :] == want
                found = jnp.where(hit, 1.0, found)
                weight = jnp.where(hit, info[k : k + 1, 2 * tok :], weight)
            pick[:, at * tok : (at + 1) * tok] = found.astype(jnp.bfloat16)
            weight_ref[at * tok : (at + 1) * tok, :] = weight.T.astype(jnp.bfloat16)

    for half in range(2):

        @pl.when(step == half)
        def _():
            own, sib = tokens[half][:tok, :], tokens[2 + half][:tok, :]
            rows = jnp.dot(pick[:, :tok], own, preferred_element_type=jnp.float32)
            rows += jnp.dot(pick[:, tok:], sib, preferred_element_type=jnp.float32)
            rows = rows.astype(jnp.bfloat16)
            pair = outs[0].shape[0]
            for i, out in enumerate(outs):
                out[...] = rows[i * pair : (i + 1) * pair]


def select(want, own, sib, top_k, parts, after):
    rows_all = want.shape[0]
    tok, tile = own[0].shape[0] - META, own[0].shape[1]
    width = 2 * tile
    pair = rows_all // parts
    kernel = functools.partial(select_kernel, top_k, parts, len(after))
    *sent, weight = call(
        kernel,
        (2,),
        [pl.BlockSpec((rows_all, 1), lambda j: (0, 0))]
        + [pl.BlockSpec((tok + META, tile), lambda j: (0, 0))] * 4,
        [pl.BlockSpec((pair, tile), lambda j: (0, j))] * parts
        + [pl.BlockSpec((2 * tok, rows_all), lambda j: (0, 0))],
        [jax.ShapeDtypeStruct((pair, width), jnp.bfloat16)] * parts
        + [jax.ShapeDtypeStruct((2 * tok, rows_all), jnp.bfloat16)],
        [pltpu.VMEM((rows_all, 2 * tok), jnp.bfloat16)],
        4 * rows_all * tok * width,
        2 * width * (2 * tok + rows_all),
        after,
        (want, *own, *sib),
        SMALL,
    )
    return sent, weight


def expert_kernel(parts, first, n_after, *refs):
    rows, (gate_ref, up_ref, down_ref) = refs[:parts], refs[parts : parts + 3]
    rest = refs[parts + 3 + n_after :]
    outs, (rows_in, hidden) = rest[:parts], rest[parts:]
    step = pl.program_id(0)
    pair = rows[0].shape[0]
    tile = gate_ref.shape[2]

    @pl.when(step == 0)
    def _():
        for i in range(parts):
            rows_in[pl.ds(i * pair, pair), :] = rows[i][...]

    @pl.when(step < first)
    def _():
        data = rows_in[...]
        gate_act = jnp.dot(data, gate_ref[0], preferred_element_type=jnp.float32)
        up_act = jnp.dot(data, up_ref[0], preferred_element_type=jnp.float32)
        act = gate_act / (1.0 + jnp.exp(-gate_act)) * up_act
        for i in range(first):

            @pl.when(step == i)
            def _():
                hidden[:, i * tile : (i + 1) * tile] = act.astype(jnp.bfloat16)

    @pl.when(step >= first)
    def _():
        made = jnp.dot(hidden[...], down_ref[0], preferred_element_type=jnp.float32)
        made = made.astype(jnp.bfloat16)
        for i in range(parts):
            outs[i][...] = made[i * pair : (i + 1) * pair]


def expert(rows, w_gate, w_up, w_down, after):
    parts = len(rows)
    pair, width = rows[0].shape
    hid = w_gate.shape[2]
    tile_h, tile_w = tile_of(hid, 256), tile_of(width, 512)
    first = hid // tile_h
    second = width // tile_w
    kernel = functools.partial(expert_kernel, parts, first, len(after))

    def early(j):
        return (0, 0, jnp.minimum(j, first - 1))

    def late(j):
        return (0, 0, jnp.maximum(j - first, 0))

    return call(
        kernel,
        (first + second,),
        [pl.BlockSpec((pair, width), lambda j: (0, 0))] * parts
        + [
            pl.BlockSpec((1, width, tile_h), early),
            pl.BlockSpec((1, width, tile_h), early),
            pl.BlockSpec((1, hid, tile_w), late),
        ],
        [pl.BlockSpec((pair, tile_w), lambda j: (0, jnp.maximum(j - first, 0)))] * parts,
        [jax.ShapeDtypeStruct((pair, width), jnp.bfloat16)] * parts,
        [
            pltpu.VMEM((parts * pair, width), jnp.bfloat16),
            pltpu.VMEM((parts * pair, hid), jnp.bfloat16),
        ],
        6 * parts * pair * hid * width,
        6 * hid * width + 4 * parts * pair * width,
        after,
        (*rows, w_gate, w_up, w_down),
        LARGE,
    )


def combine_kernel(parts, n_after, weight_ref, *refs):
    home = refs[:parts]
    own_ref, left_ref, right_ref, rows = refs[parts + n_after :]
    step = pl.program_id(0)
    tok = own_ref.shape[0]
    pair = home[0].shape[0]
    for i in range(parts):
        rows[pl.ds(i * pair, pair), :] = home[i][...]
    mixed = jnp.dot(weight_ref[...], rows[...], preferred_element_type=jnp.float32)
    own_ref[...] = mixed[:tok]
    for half, sib_ref in enumerate((left_ref, right_ref)):

        @pl.when(step == half)
        def _():
            sib_ref[...] = mixed[tok:].astype(jnp.bfloat16)


def combine(weight, home, after):
    parts = len(home)
    both, rows_all = weight.shape
    tok = both // 2
    pair, width = home[0].shape
    tile = width // 2
    half = pl.BlockSpec((tok, tile), lambda j: (0, 0))
    return call(
        functools.partial(combine_kernel, parts, len(after)),
        (2,),
        [pl.BlockSpec((both, rows_all), lambda j: (0, 0))]
        + [pl.BlockSpec((pair, tile), lambda j: (0, j))] * parts,
        [pl.BlockSpec((tok, tile), lambda j: (0, j)), half, half],
        [jax.ShapeDtypeStruct((tok, width), jnp.float32)]
        + [jax.ShapeDtypeStruct((tok, tile), jnp.bfloat16)] * 2,
        [pltpu.VMEM((rows_all, tile), jnp.bfloat16)],
        2 * rows_all * both * width,
        2 * width * (both * 2 + rows_all),
        after,
        (weight, *home),
        SMALL,
    )


def pass_kernel(count, n_after, *refs):
    outs = refs[count + n_after :]
    for i in range(count):
        outs[i][...] = refs[i][...]


def passed(values, after):
    rows, width = values[0].shape
    tile = tile_of(width, width // 2)
    count = len(values)
    return call(
        functools.partial(pass_kernel, count, len(after)),
        (width // tile,),
        [pl.BlockSpec((rows, tile), lambda j: (0, j))] * count,
        [pl.BlockSpec((rows, tile), lambda j: (0, j))] * count,
        [jax.ShapeDtypeStruct(value.shape, value.dtype) for value in values],
        [],
        1,
        4 * count * rows * width,
        after,
        tuple(values),
        SMALL,
    )


def relay_kernel(chooser, copies, whole, count, n_after, plane_ref, *refs):
    step = pl.program_id(0)
    values = [ref[...] for ref in refs[:count]]
    left_ref, right_ref, *outs = refs[count + n_after :]
    kept = chooser(plane_ref[0], *values)
    for half, ref in enumerate((left_ref, right_ref)):

        @pl.when(step == half)
        def _():
            ref[...] = kept

    for value, out in zip([kept] * whole + values[:copies], outs):
        out[...] = value


def relay(chooser, plane, values, whole, copies, after):
    rows, width = values[0].shape
    tile = width // 2
    count = len(values)
    block = pl.BlockSpec((rows, tile), lambda j: (0, j))
    half = pl.BlockSpec((rows, tile), lambda j: (0, 0))
    return call(
        functools.partial(relay_kernel, chooser, copies, whole, count, len(after)),
        (2,),
        [pl.BlockSpec(memory_space=pltpu.SMEM)] + [block] * count,
        [half, half] + [block] * (whole + copies),
        [jax.ShapeDtypeStruct((rows, tile), jnp.bfloat16)] * 2
        + [jax.ShapeDtypeStruct((rows, width), jnp.bfloat16)] * (whole + copies),
        [],
        1,
        2 * (count + 1 + whole + copies) * rows * width,
        after,
        (plane, *values),
        SMALL,
    )


def add_kernel(n_after, own_ref, left_ref, right_ref, *rest):
    out_ref = rest[n_after]
    tok, half = left_ref.shape
    for at, ref in enumerate((left_ref, right_ref)):
        part = own_ref[:, at * half : (at + 1) * half] + ref[...].astype(jnp.float32)
        out_ref[:tok, at * half : (at + 1) * half] = part.astype(out_ref.dtype)
    if out_ref.shape[0] > tok:
        rest_of = out_ref.shape[0] - tok
        out_ref[tok:, :] = jnp.zeros((rest_of, 2 * half), out_ref.dtype)


def added(own, sib, after, extra=0):
    tok, width = own.shape
    half = pl.BlockSpec((tok, width // 2), lambda j: (0, 0))
    whole = pl.BlockSpec((tok, width), lambda j: (0, 0))
    return call(
        functools.partial(add_kernel, len(after)),
        (1,),
        [whole, half, half],
        pl.BlockSpec((tok + extra, width), lambda j: (0, 0)),
        jax.ShapeDtypeStruct((tok + extra, width), jnp.bfloat16),
        [],
        tok * width,
        8 * tok * width,
        after,
        (own, *sib),
        SMALL,
    )


def route(affinity, group_ids, expert_ids, experts_all, local_count):
    tok_rows, top_k = expert_ids.shape
    pair_size = top_k // group_ids.shape[1]
    gate_weights = (2.5 * affinity / jnp.sum(affinity, axis=1, keepdims=True)).astype(jnp.bfloat16)
    chosen = jnp.repeat(group_ids, pair_size, axis=1)
    is_valid = expert_ids // local_count == chosen
    mixing = jnp.where(is_valid, gate_weights, jnp.zeros((), jnp.bfloat16)).T
    target = jnp.where(is_valid, expert_ids, -1).T
    is_member = target[:, None, :] == jnp.arange(experts_all)[None, :, None]
    member = jnp.sum(is_member.astype(jnp.float32), axis=0).astype(jnp.bfloat16)
    earlier = (jnp.arange(tok_rows)[:, None] < jnp.arange(tok_rows)[None, :]).astype(jnp.bfloat16)
    before = jnp.dot(member, earlier, preferred_element_type=jnp.float32)
    slot = jnp.sum(jnp.where(is_member, before[None], 0.0), axis=1)
    info = [target.astype(jnp.bfloat16), slot.astype(jnp.bfloat16), mixing]
    return jnp.pad(jnp.concatenate(info, axis=1), ((0, META - top_k), (0, 0)))


def shards(dims, hidden_states, affinity, group_ids, expert_ids, w_gate, w_up, w_down):
    ys, cs, zs, xs = dims
    tok_rows, width = hidden_states.shape
    top_k = expert_ids.shape[1]
    local_count = zs * xs
    experts_all = ys * cs * local_count
    most_rows = 5 * tok_rows * top_k // (4 * experts_all)
    me_y, me_c = lax.axis_index("row"), lax.axis_index("core")
    me_z, me_x = lax.axis_index("plane"), lax.axis_index("column")
    plane = me_z.astype(jnp.int32).reshape(1)

    meta = route(affinity, group_ids, expert_ids, experts_all, local_count)
    meta = jnp.pad(meta, ((0, 0), (0, width - meta.shape[1])))
    payload = jnp.concatenate([hidden_states, meta], axis=0)
    middle = width // 2
    payload_halves = [
        jnp.concatenate([hidden_states[:, :middle], meta[:, :middle]], axis=0),
        jnp.concatenate([hidden_states[:, middle:], meta[:, middle:]], axis=0),
    ]

    rel = [(dx, dy) for dx in range(xs) for dy in range(ys)]
    parts = len(rel)
    pair = -(-cs * most_rows // 16) * 16
    wanted = jnp.stack(
        [((me_y ^ dy) * cs + me_c) * local_count + me_z * xs + (me_x ^ dx) for dx, dy in rel]
    ).astype(jnp.float32)
    row = jnp.arange(pair)
    in_pair = jnp.where(
        row < cs * most_rows, row // most_rows * OFFSET + row % most_rows, -2 * OFFSET
    ).astype(jnp.float32)
    want = (wanted[:, None] * tok_rows + in_pair[None, :]).reshape(-1, 1)

    tokens, siblings, arrived, weights, made, halves, sums = {}, {}, {}, {}, {}, {}, {}
    last = []

    def hop(value, step, sources):
        return lax.ppermute(value, "plane", [(z, z + step) for z in sources])

    def have(dz, halves):
        tokens[dz] = halves
        siblings[dz] = [swap(half, "core", 1) for half in halves]

    def relayed(dz, chooser, values, whole, copies, *after):
        left, right, *outs = relay(chooser, plane, values, whole, copies, last + list(after))
        last[:] = [left]
        have(dz, (left, right))
        return outs

    def in_plane(values):
        return [
            part if (dx, dy) == (0, 0) else swap_in_plane(part, dx, dy)
            for part, (dx, dy) in zip(values, rel)
        ]

    def send_free(dz):
        own, sib = halves[dz]
        part = own + jnp.concatenate(sib, axis=1).astype(jnp.float32)
        sums[dz] = swap(part.astype(jnp.bfloat16), "plane", dz)

    def tick(*after):
        (out,) = passed([meta[:, : 3 * tok_rows]], last + list(after))
        last[:] = [out]

    def dispatch(dz, *after):
        sent, weights[dz] = select(
            want, tokens[dz], siblings[dz], top_k, parts, last + list(after)
        )
        last[:] = [weights[dz]]
        arrived[dz] = in_plane(sent)

    def apply(dz, *after):
        made[dz] = expert(arrived[dz], w_gate, w_up, w_down, last + list(after))
        last[:] = [made[dz][0]]

    def give_back(dz, late=False):
        sent = made[dz]
        if late:
            sent = passed(sent, last)
            last[:] = [sent[0]]
        halves[dz] = in_plane(sent)

    def collect(dz, *after, whole=False):
        own, *sib = combine(weights[dz], halves[dz], last + list(after))
        last[:] = [sib[0]]
        if whole:
            came = swap(jnp.concatenate(sib, axis=1), "core", 1)
            halves[dz] = own, [came[:, :middle], came[:, middle:]]
            return
        halves[dz] = own, [swap(half, "core", 1) for half in sib]

    def send_home(dz, *after, extra=0):
        part = added(*halves[dz], last + list(after), extra)
        last[:] = [part]
        sums[dz] = swap(part, "plane", dz)

    up1, down1 = hop(payload, 1, (0, 1, 2)), hop(payload, -1, (1, 2, 3))
    have(0, payload_halves)
    dispatch(0)
    up1, down1 = relayed(
        1, lambda z, u, d: jnp.where(z % 2 == 1, u, d), [up1, down1], 0, 2
    )
    up2, down2 = hop(up1, 1, (1, 2)), hop(down1, -1, (1, 2))
    dispatch(1, *arrived[0][1:3])
    apply(0)
    (second,) = relayed(
        2, lambda z, u, d: jnp.where(z >= 2, u, d), [up2, down2], 1, 0
    )
    ends = lax.ppermute(second, "plane", [(1, 0), (2, 3)])
    dispatch(2, *arrived[1][1:3])
    apply(1)
    relayed(
        3,
        lambda z, u, d, e: jnp.where(z == 1, d, jnp.where(z == 2, u, e)),
        [up1, down1, ends],
        0,
        0,
    )
    dispatch(3, *arrived[2][1:3])
    apply(2)
    give_back(2)
    apply(3)
    give_back(3)
    collect(2)
    send_home(2)
    give_back(1, late=True)
    collect(3, whole=True)
    tick(sums[2])
    send_home(3)
    give_back(0, late=True)
    collect(1)
    send_free(1)
    tick(sums[3])
    collect(0)
    own, sib = halves[0]
    sums[0] = own + jnp.concatenate(sib, axis=1).astype(jnp.float32)
    total = sums[0]
    for dz in range(1, zs):
        total = total + sums[dz][:tok_rows].astype(jnp.float32)
    return total.astype(jnp.bfloat16)


def solution(mesh):
    dims = plan(mesh.shape)
    finer = jax.sharding.Mesh(mesh.devices.reshape(dims), ALL)

    def body(*args):
        return shards(dims, *args)

    placed = (P(ALL, None),) * 4 + (P(ALL, None, None),) * 3
    return jax.shard_map(body, mesh=finer, in_specs=placed, out_specs=P(ALL, None), check_vma=False)
```

```python
import functools

import jax
import jax.numpy as jnp
from jax import lax
from jax.experimental import pallas as pl
from jax.experimental.pallas import tpu as pltpu
from jax.sharding import PartitionSpec as P

ALL = ("row", "core", "plane", "column")
PLANE = ("row", "core", "column")
META = 16
OFFSET = 1 << 20
SMALL = 24 * 1024 * 1024
LARGE = 52 * 1024 * 1024


def plan(mesh_shape):
    group_count, local_count = mesh_shape["group"], mesh_shape["local"]
    cores = 2
    planes = 1
    while planes * planes < local_count:
        planes *= 2
    return group_count // cores, cores, planes, local_count // planes


def swap(value, axis, delta):
    size = lax.axis_size(axis)
    return lax.ppermute(value, axis, [(i, i ^ delta) for i in range(size)])


def swap_in_plane(value, dx, dy):
    xs, ys = lax.axis_size("column"), lax.axis_size("row")
    cs = lax.axis_size("core")
    pairs = [
        ((y * cs + c) * xs + x, ((y ^ dy) * cs + c) * xs + (x ^ dx))
        for y in range(ys)
        for c in range(cs)
        for x in range(xs)
    ]
    return lax.ppermute(value, PLANE, pairs)


def tile_of(width, most):
    best = 128
    for size in range(128, most + 1, 128):
        if width % size == 0:
            best = size
    return best


def call(
    kernel, grid, in_specs, out_specs, out_shape, scratch, flops, nbytes, after, operands, limit
):
    return pl.pallas_call(
        kernel,
        grid=grid,
        in_specs=list(in_specs) + [pl.BlockSpec(memory_space=pl.ANY)] * len(after),
        out_specs=out_specs,
        out_shape=out_shape,
        scratch_shapes=scratch,
        cost_estimate=pl.CostEstimate(flops=flops, bytes_accessed=nbytes, transcendentals=0),
        compiler_params=pltpu.CompilerParams(
            dimension_semantics=("arbitrary",), vmem_limit_bytes=limit
        ),
    )(*operands, *after)


def select_kernel(top_k, parts, n_after, want_ref, *refs):
    tokens = refs[:4]
    rest = refs[4 + n_after :]
    outs, (weight_ref, pick) = rest[:parts], rest[parts:]
    step = pl.program_id(0)
    tok = tokens[0].shape[0] - META

    @pl.when(step == 0)
    def _():
        want = want_ref[...]
        rows_all = want.shape[0]
        for at, ref in enumerate(tokens[::2]):
            info = ref[tok : tok + META, : 3 * tok].astype(jnp.float32)
            code = info[:, :tok] * tok + info[:, tok : 2 * tok] + float(at * OFFSET)
            found = jnp.zeros((rows_all, tok), jnp.float32)
            weight = jnp.zeros((rows_all, tok), jnp.float32)
            for k in range(top_k):
                hit = code[k : k + 1, :] == want
                found = jnp.where(hit, 1.0, found)
                weight = jnp.where(hit, info[k : k + 1, 2 * tok :], weight)
            pick[:, at * tok : (at + 1) * tok] = found.astype(jnp.bfloat16)
            weight_ref[at * tok : (at + 1) * tok, :] = weight.T.astype(jnp.bfloat16)

    for half in range(2):

        @pl.when(step == half)
        def _():
            own, sib = tokens[half][:tok, :], tokens[2 + half][:tok, :]
            rows = jnp.dot(pick[:, :tok], own, preferred_element_type=jnp.float32)
            rows += jnp.dot(pick[:, tok:], sib, preferred_element_type=jnp.float32)
            rows = rows.astype(jnp.bfloat16)
            pair = outs[0].shape[0]
            for i, out in enumerate(outs):
                out[...] = rows[i * pair : (i + 1) * pair]


def select(want, own, sib, top_k, parts, after):
    rows_all = want.shape[0]
    tok, tile = own[0].shape[0] - META, own[0].shape[1]
    width = 2 * tile
    pair = rows_all // parts
    kernel = functools.partial(select_kernel, top_k, parts, len(after))
    *sent, weight = call(
        kernel,
        (2,),
        [pl.BlockSpec((rows_all, 1), lambda j: (0, 0))]
        + [pl.BlockSpec((tok + META, tile), lambda j: (0, 0))] * 4,
        [pl.BlockSpec((pair, tile), lambda j: (0, j))] * parts
        + [pl.BlockSpec((2 * tok, rows_all), lambda j: (0, 0))],
        [jax.ShapeDtypeStruct((pair, width), jnp.bfloat16)] * parts
        + [jax.ShapeDtypeStruct((2 * tok, rows_all), jnp.bfloat16)],
        [pltpu.VMEM((rows_all, 2 * tok), jnp.bfloat16)],
        4 * rows_all * tok * width,
        2 * width * (2 * tok + rows_all),
        after,
        (want, *own, *sib),
        SMALL,
    )
    return sent, weight


def expert_kernel(parts, first, n_after, *refs):
    rows, (gate_ref, up_ref, down_ref) = refs[:parts], refs[parts : parts + 3]
    rest = refs[parts + 3 + n_after :]
    outs, (rows_in, hidden) = rest[:parts], rest[parts:]
    step = pl.program_id(0)
    pair = rows[0].shape[0]
    tile = gate_ref.shape[2]

    @pl.when(step == 0)
    def _():
        for i in range(parts):
            rows_in[pl.ds(i * pair, pair), :] = rows[i][...]

    @pl.when(step < first)
    def _():
        data = rows_in[...]
        gate_act = jnp.dot(data, gate_ref[0], preferred_element_type=jnp.float32)
        up_act = jnp.dot(data, up_ref[0], preferred_element_type=jnp.float32)
        act = gate_act / (1.0 + jnp.exp(-gate_act)) * up_act
        for i in range(first):

            @pl.when(step == i)
            def _():
                hidden[:, i * tile : (i + 1) * tile] = act.astype(jnp.bfloat16)

    @pl.when(step >= first)
    def _():
        made = jnp.dot(hidden[...], down_ref[0], preferred_element_type=jnp.float32)
        made = made.astype(jnp.bfloat16)
        for i in range(parts):
            outs[i][...] = made[i * pair : (i + 1) * pair]


def expert(rows, w_gate, w_up, w_down, after):
    parts = len(rows)
    pair, width = rows[0].shape
    hid = w_gate.shape[2]
    tile_h, tile_w = tile_of(hid, 256), tile_of(width, 512)
    first = hid // tile_h
    second = width // tile_w
    kernel = functools.partial(expert_kernel, parts, first, len(after))

    def early(j):
        return (0, 0, jnp.minimum(j, first - 1))

    def late(j):
        return (0, 0, jnp.maximum(j - first, 0))

    return call(
        kernel,
        (first + second,),
        [pl.BlockSpec((pair, width), lambda j: (0, 0))] * parts
        + [
            pl.BlockSpec((1, width, tile_h), early),
            pl.BlockSpec((1, width, tile_h), early),
            pl.BlockSpec((1, hid, tile_w), late),
        ],
        [pl.BlockSpec((pair, tile_w), lambda j: (0, jnp.maximum(j - first, 0)))] * parts,
        [jax.ShapeDtypeStruct((pair, width), jnp.bfloat16)] * parts,
        [
            pltpu.VMEM((parts * pair, width), jnp.bfloat16),
            pltpu.VMEM((parts * pair, hid), jnp.bfloat16),
        ],
        6 * parts * pair * hid * width,
        6 * hid * width + 4 * parts * pair * width,
        after,
        (*rows, w_gate, w_up, w_down),
        LARGE,
    )


def combine_kernel(parts, n_after, weight_ref, *refs):
    home = refs[:parts]
    own_ref, left_ref, right_ref, rows = refs[parts + n_after :]
    step = pl.program_id(0)
    tok = own_ref.shape[0]
    pair = home[0].shape[0]
    for i in range(parts):
        rows[pl.ds(i * pair, pair), :] = home[i][...]
    mixed = jnp.dot(weight_ref[...], rows[...], preferred_element_type=jnp.float32)
    own_ref[...] = mixed[:tok]
    for half, sib_ref in enumerate((left_ref, right_ref)):

        @pl.when(step == half)
        def _():
            sib_ref[...] = mixed[tok:].astype(jnp.bfloat16)


def combine(weight, home, after):
    parts = len(home)
    both, rows_all = weight.shape
    tok = both // 2
    pair, width = home[0].shape
    tile = width // 2
    half = pl.BlockSpec((tok, tile), lambda j: (0, 0))
    return call(
        functools.partial(combine_kernel, parts, len(after)),
        (2,),
        [pl.BlockSpec((both, rows_all), lambda j: (0, 0))]
        + [pl.BlockSpec((pair, tile), lambda j: (0, j))] * parts,
        [pl.BlockSpec((tok, tile), lambda j: (0, j)), half, half],
        [jax.ShapeDtypeStruct((tok, width), jnp.float32)]
        + [jax.ShapeDtypeStruct((tok, tile), jnp.bfloat16)] * 2,
        [pltpu.VMEM((rows_all, tile), jnp.bfloat16)],
        2 * rows_all * both * width,
        2 * width * (both * 2 + rows_all),
        after,
        (weight, *home),
        SMALL,
    )


def pass_kernel(count, n_after, *refs):
    outs = refs[count + n_after :]
    for i in range(count):
        outs[i][...] = refs[i][...]


def passed(values, after):
    rows, width = values[0].shape
    tile = tile_of(width, width // 2)
    count = len(values)
    return call(
        functools.partial(pass_kernel, count, len(after)),
        (width // tile,),
        [pl.BlockSpec((rows, tile), lambda j: (0, j))] * count,
        [pl.BlockSpec((rows, tile), lambda j: (0, j))] * count,
        [jax.ShapeDtypeStruct(value.shape, value.dtype) for value in values],
        [],
        1,
        4 * count * rows * width,
        after,
        tuple(values),
        SMALL,
    )


def relay_kernel(chooser, copies, whole, count, n_after, plane_ref, *refs):
    step = pl.program_id(0)
    values = [ref[...] for ref in refs[:count]]
    left_ref, right_ref, *outs = refs[count + n_after :]
    kept = chooser(plane_ref[0], *values)
    for half, ref in enumerate((left_ref, right_ref)):

        @pl.when(step == half)
        def _():
            ref[...] = kept

    for value, out in zip([kept] * whole + values[:copies], outs):
        out[...] = value


def relay(chooser, plane, values, whole, copies, after):
    rows, width = values[0].shape
    tile = width // 2
    count = len(values)
    block = pl.BlockSpec((rows, tile), lambda j: (0, j))
    half = pl.BlockSpec((rows, tile), lambda j: (0, 0))
    return call(
        functools.partial(relay_kernel, chooser, copies, whole, count, len(after)),
        (2,),
        [pl.BlockSpec(memory_space=pltpu.SMEM)] + [block] * count,
        [half, half] + [block] * (whole + copies),
        [jax.ShapeDtypeStruct((rows, tile), jnp.bfloat16)] * 2
        + [jax.ShapeDtypeStruct((rows, width), jnp.bfloat16)] * (whole + copies),
        [],
        1,
        2 * (count + 1 + whole + copies) * rows * width,
        after,
        (plane, *values),
        SMALL,
    )


def add_kernel(n_after, own_ref, left_ref, right_ref, *rest):
    out_ref = rest[n_after]
    tok, half = left_ref.shape
    for at, ref in enumerate((left_ref, right_ref)):
        part = own_ref[:, at * half : (at + 1) * half] + ref[...].astype(jnp.float32)
        out_ref[:tok, at * half : (at + 1) * half] = part.astype(out_ref.dtype)
    if out_ref.shape[0] > tok:
        rest_of = out_ref.shape[0] - tok
        out_ref[tok:, :] = jnp.zeros((rest_of, 2 * half), out_ref.dtype)


def added(own, sib, after, extra=0):
    tok, width = own.shape
    half = pl.BlockSpec((tok, width // 2), lambda j: (0, 0))
    whole = pl.BlockSpec((tok, width), lambda j: (0, 0))
    return call(
        functools.partial(add_kernel, len(after)),
        (1,),
        [whole, half, half],
        pl.BlockSpec((tok + extra, width), lambda j: (0, 0)),
        jax.ShapeDtypeStruct((tok + extra, width), jnp.bfloat16),
        [],
        tok * width,
        8 * tok * width,
        after,
        (own, *sib),
        SMALL,
    )


def route(affinity, group_ids, expert_ids, experts_all, local_count):
    tok_rows, top_k = expert_ids.shape
    pair_size = top_k // group_ids.shape[1]
    gate_weights = (2.5 * affinity / jnp.sum(affinity, axis=1, keepdims=True)).astype(jnp.bfloat16)
    chosen = jnp.repeat(group_ids, pair_size, axis=1)
    is_valid = expert_ids // local_count == chosen
    mixing = jnp.where(is_valid, gate_weights, jnp.zeros((), jnp.bfloat16)).T
    target = jnp.where(is_valid, expert_ids, -1).T
    is_member = target[:, None, :] == jnp.arange(experts_all)[None, :, None]
    member = jnp.sum(is_member.astype(jnp.float32), axis=0).astype(jnp.bfloat16)
    earlier = (jnp.arange(tok_rows)[:, None] < jnp.arange(tok_rows)[None, :]).astype(jnp.bfloat16)
    before = jnp.dot(member, earlier, preferred_element_type=jnp.float32)
    slot = jnp.sum(jnp.where(is_member, before[None], 0.0), axis=1)
    info = [target.astype(jnp.bfloat16), slot.astype(jnp.bfloat16), mixing]
    return jnp.pad(jnp.concatenate(info, axis=1), ((0, META - top_k), (0, 0)))


def shards(dims, hidden_states, affinity, group_ids, expert_ids, w_gate, w_up, w_down):
    ys, cs, zs, xs = dims
    tok_rows, width = hidden_states.shape
    top_k = expert_ids.shape[1]
    local_count = zs * xs
    experts_all = ys * cs * local_count
    most_rows = 5 * tok_rows * top_k // (4 * experts_all)
    me_y, me_c = lax.axis_index("row"), lax.axis_index("core")
    me_z, me_x = lax.axis_index("plane"), lax.axis_index("column")
    plane = me_z.astype(jnp.int32).reshape(1)

    meta = route(affinity, group_ids, expert_ids, experts_all, local_count)
    meta = jnp.pad(meta, ((0, 0), (0, width - meta.shape[1])))
    payload = jnp.concatenate([hidden_states, meta], axis=0)
    middle = width // 2
    payload_halves = [
        jnp.concatenate([hidden_states[:, :middle], meta[:, :middle]], axis=0),
        jnp.concatenate([hidden_states[:, middle:], meta[:, middle:]], axis=0),
    ]

    rel = [(dx, dy) for dx in range(xs) for dy in range(ys)]
    parts = len(rel)
    pair = -(-cs * most_rows // 16) * 16
    wanted = jnp.stack(
        [((me_y ^ dy) * cs + me_c) * local_count + me_z * xs + (me_x ^ dx) for dx, dy in rel]
    ).astype(jnp.float32)
    row = jnp.arange(pair)
    in_pair = jnp.where(
        row < cs * most_rows, row // most_rows * OFFSET + row % most_rows, -2 * OFFSET
    ).astype(jnp.float32)
    want = (wanted[:, None] * tok_rows + in_pair[None, :]).reshape(-1, 1)

    tokens, siblings, arrived, weights, made, halves, sums = {}, {}, {}, {}, {}, {}, {}
    last = []

    def hop(value, step, sources):
        return lax.ppermute(value, "plane", [(z, z + step) for z in sources])

    def have(dz, halves):
        tokens[dz] = halves
        siblings[dz] = [swap(half, "core", 1) for half in halves]

    def relayed(dz, chooser, values, whole, copies, *after):
        left, right, *outs = relay(chooser, plane, values, whole, copies, last + list(after))
        last[:] = [left]
        have(dz, (left, right))
        return outs

    def in_plane(values):
        return [
            part if (dx, dy) == (0, 0) else swap_in_plane(part, dx, dy)
            for part, (dx, dy) in zip(values, rel)
        ]

    def send_free(dz):
        own, sib = halves[dz]
        part = own + jnp.concatenate(sib, axis=1).astype(jnp.float32)
        sums[dz] = swap(part.astype(jnp.bfloat16), "plane", dz)

    def tick(*after):
        (out,) = passed([meta[:, : 3 * tok_rows]], last + list(after))
        last[:] = [out]

    def dispatch(dz, *after):
        sent, weights[dz] = select(
            want, tokens[dz], siblings[dz], top_k, parts, last + list(after)
        )
        last[:] = [weights[dz]]
        arrived[dz] = in_plane(sent)

    def apply(dz, *after):
        made[dz] = expert(arrived[dz], w_gate, w_up, w_down, last + list(after))
        last[:] = [made[dz][0]]

    def give_back(dz, late=False):
        sent = made[dz]
        if late:
            sent = passed(sent, last)
            last[:] = [sent[0]]
        halves[dz] = in_plane(sent)

    def collect(dz, *after, whole=False):
        own, *sib = combine(weights[dz], halves[dz], last + list(after))
        last[:] = [sib[0]]
        if whole:
            came = swap(jnp.concatenate(sib, axis=1), "core", 1)
            halves[dz] = own, [came[:, :middle], came[:, middle:]]
            return
        halves[dz] = own, [swap(half, "core", 1) for half in sib]

    def send_home(dz, *after, extra=0):
        part = added(*halves[dz], last + list(after), extra)
        last[:] = [part]
        sums[dz] = swap(part, "plane", dz)

    up1, down1 = hop(payload, 1, (0, 1, 2)), hop(payload, -1, (1, 2, 3))
    have(0, payload_halves)
    dispatch(0)
    up1, down1 = relayed(
        1, lambda z, u, d: jnp.where(z % 2 == 1, u, d), [up1, down1], 0, 2
    )
    up2, down2 = hop(up1, 1, (1, 2)), hop(down1, -1, (1, 2))
    dispatch(1, arrived[0][1])
    apply(0)
    (second,) = relayed(
        2, lambda z, u, d: jnp.where(z >= 2, u, d), [up2, down2], 1, 0
    )
    ends = lax.ppermute(second, "plane", [(1, 0), (2, 3)])
    dispatch(2, arrived[1][1])
    apply(1)
    relayed(
        3,
        lambda z, u, d, e: jnp.where(z == 1, d, jnp.where(z == 2, u, e)),
        [up1, down1, ends],
        0,
        0,
    )
    dispatch(3, arrived[2][1])
    apply(2)
    give_back(2)
    apply(3)
    give_back(3)
    collect(2)
    send_home(2)
    give_back(1, late=True)
    collect(3, whole=True)
    tick(sums[2])
    send_home(3)
    give_back(0, late=True)
    collect(1)
    send_free(1)
    tick(sums[3])
    collect(0)
    own, sib = halves[0]
    sums[0] = own + jnp.concatenate(sib, axis=1).astype(jnp.float32)
    total = sums[0]
    for dz in range(1, zs):
        total = total + sums[dz][:tok_rows].astype(jnp.float32)
    return total.astype(jnp.bfloat16)


def solution(mesh):
    dims = plan(mesh.shape)
    finer = jax.sharding.Mesh(mesh.devices.reshape(dims), ALL)

    def body(*args):
        return shards(dims, *args)

    placed = (P(ALL, None),) * 4 + (P(ALL, None, None),) * 3
    return jax.shard_map(body, mesh=finer, in_specs=placed, out_specs=P(ALL, None), check_vma=False)
```
